1024 devices in a mesh: expert: 16 (over y, x), dp: 64 (over z, core).
Axes of the slice: x: 4, y: 4, z: 32, core: 2. Of those that a mesh axis runs over, the one named last changes fastest.
Arguments:
- tokens: bfloat16 [131072, 2048], P(('expert', 'dp')), may hold values from -6 to 6
- out_grad: bfloat16 [131072, 2048], P(('expert', 'dp')), may hold values from -6 to 6
- proj_in: bfloat16 [16, 2048, 512], P('expert'), may hold values from -0.125 to 0.125
- proj_out: bfloat16 [16, 512, 2048], P('expert'), may hold values from -0.25 to 0.25
- picked: int32 [1024, 16, 4], P(('expert', 'dp')), may hold values from 0 to 127, as said below
- gate_values: float32 [1024, 16, 4], P(('expert', 'dp')), may hold values from 0.1 to 1
Outputs:
- layer_out: bfloat16 [131072, 2048], P(('expert', 'dp'))
- token_grads: bfloat16 [131072, 2048], P(('expert', 'dp'))
- gate_grads: float32 [1024, 16, 4], P(('expert', 'dp'))
- grad_proj_in: float32 [16, 2048, 512], P('expert', 'dp')
The draws below stay inside these ranges and needn't reach their ends.
Inputs may be any that keep to these rules, and one draw needn't show every extreme that they name: `picked`: for each group and expert the 4 entries are distinct positions among the group's 128 tokens.
All inputs are finite; a program needn't handle non-finite values.
Results may differ from the reference program's by a relative error of at most 0.0085.
Values may be sent and summed in bfloat16 or wider, within the bound.
A program may use at most 32 MiB of HBM per device.

```python
import math
import jax
import jax.numpy as jnp
from jax import lax

D = 2048
F = 512
GROUP = 128
CAP = 4
EXPERTS = 16
GROUPS = 1024
TOKENS = 131072


def draw_picked(key, part):
    key = jax.random.fold_in(key, 7)
    row_count = GROUPS * EXPERTS
    all_keys = jax.random.split(key, row_count)
    row_perms = jax.vmap(lambda one_key: jax.random.permutation(one_key, GROUP))(all_keys)[:, :CAP].astype(jnp.int32)
    lead_value = row_perms[0, 0]
    row_index = jnp.arange(row_count, dtype=jnp.int32)
    row_shift = jnp.where(row_index == 0, GROUP - 1 - lead_value, 0).astype(jnp.int32)
    chosen = (row_perms + row_shift[:, None]) % GROUP
    return chosen.reshape(GROUPS, EXPERTS, CAP).astype(jnp.int32)


def levels(own_key, dims, cuts, least, high):
    def one(dim, blocks):
        draws = jax.random.uniform(jax.random.fold_in(jax.random.fold_in(own_key, 6), dim), (blocks,), jnp.float32, least / len(cuts), high / len(cuts))
        return jnp.repeat(jnp.exp(draws), dims[dim] // blocks).reshape((-1,) + (1,) * (len(dims) - dim - 1))

    loudness = one(*cuts[0])
    for cut in cuts[1:]:
        loudness = loudness * one(*cut)
    return loudness


def normal_values(own_key, extent, width, reach, cuts=(), kind=jnp.bfloat16):
    drawn = jax.random.normal(own_key, extent, jnp.float32) * width
    if len(cuts) > 0:
        drawn = levels(own_key, extent, cuts, -0.22, 0.18) * drawn
    return jnp.clip(drawn, min=-reach, max=reach).astype(kind)


def setup_inputs(seed: int = 0) -> dict:
    streams_of = jax.random.split(jax.random.key(seed), 7)
    tokens = normal_values(streams_of[0], (TOKENS, D), 1.0, 6.0, ((0, 1024),))
    out_grad = normal_values(streams_of[1], (TOKENS, D), 1.0, 6.0, ((0, 1024),))
    proj_in = normal_values(streams_of[2], (EXPERTS, D, F), D ** -0.5, 0.125, ((0, 16),))
    proj_out = normal_values(streams_of[3], (EXPERTS, F, D), F ** -0.5, 0.25, ((0, 16),))
    picked = draw_picked(jax.random.fold_in(streams_of[6], 71), 0)
    gate_values = jnp.clip(jnp.exp(math.log(1.0) - 2.3025851 * jax.random.uniform(streams_of[5], (GROUPS, EXPERTS, CAP), jnp.float32) ** levels(streams_of[5], (GROUPS, EXPERTS, CAP), ((0, 1024),), -0.2, 0.2)), 0.1, 1.0)
    return {"tokens": tokens, "out_grad": out_grad, "proj_in": proj_in, "proj_out": proj_out, "picked": picked, "gate_values": gate_values}


def gelu_parts(hidden_pre):
    normal_cdf = 0.5 * (1.0 + lax.erf(hidden_pre * (1.0 / math.sqrt(2.0))))
    density = jnp.exp(-0.5 * hidden_pre * hidden_pre) * (1.0 / math.sqrt(2.0 * math.pi))
    return (hidden_pre * normal_cdf, normal_cdf + hidden_pre * density)

def device_sum(left, right):
    return jnp.einsum('rk,rf->kf', left.astype(jnp.float32), right.astype(jnp.float32), precision=lax.Precision.HIGHEST)

def reference(tokens, out_grad, proj_in, proj_out, picked, gate_values):
    starts = (jnp.arange(GROUPS, dtype=jnp.int32) * GROUP)[:, None]

    def per_expert(carry, expert):
        out_acc, grad_acc = carry
        token_index = (starts + picked[:, expert, :]).reshape(-1).astype(jnp.int32)
        gate_col = gate_values[:, expert, :].reshape(-1)
        rows_in = tokens[token_index]
        grad_rows = out_grad[token_index]
        weight_a = proj_in[expert]
        weight_b = proj_out[expert]
        hidden_pre = jnp.dot(rows_in, weight_a, preferred_element_type=jnp.float32)
        activation, gelu_slope = gelu_parts(hidden_pre)
        hidden = activation.astype(jnp.bfloat16)
        expert_out = jnp.dot(hidden, weight_b, preferred_element_type=jnp.float32).astype(jnp.bfloat16)
        out_acc = out_acc.at[token_index].add(gate_col[:, None] * expert_out.astype(jnp.float32))
        gate_grad = lax.optimization_barrier(jnp.sum(grad_rows.astype(jnp.float32) * expert_out.astype(jnp.float32), axis=1)).reshape(GROUPS, CAP)
        scaled = (gate_col[:, None] * grad_rows.astype(jnp.float32)).astype(jnp.bfloat16)
        back_act = jnp.dot(scaled, weight_b.T, preferred_element_type=jnp.float32)
        back_pre = (back_act * gelu_slope).astype(jnp.bfloat16)
        input_rows = jnp.dot(back_pre, weight_a.T, preferred_element_type=jnp.float32).astype(jnp.bfloat16)
        grad_acc = grad_acc.at[token_index].add(input_rows.astype(jnp.float32))
        grad_in = device_sum(rows_in, back_pre)
        return ((out_acc, grad_acc), (gate_grad, grad_in))
    zeros_init = jnp.zeros((TOKENS, D), jnp.float32)
    (out_acc, grad_acc), (gate_stack, grad_proj_in) = lax.scan(per_expert, (zeros_init, zeros_init), jnp.arange(EXPERTS, dtype=jnp.int32))
    gate_grads = jnp.transpose(gate_stack, (1, 0, 2))
    return (out_acc.astype(jnp.bfloat16), grad_acc.astype(jnp.bfloat16), gate_grads, grad_proj_in)
```

```python
import functools
import math

import jax
import jax.numpy as jnp
from jax import lax
from jax.experimental import pallas as pl
from jax.experimental.pallas import tpu as pltpu
from jax.sharding import PartitionSpec as P

MESH = pl.DeviceIdType.MESH
BF = jnp.bfloat16
F32 = jnp.float32
E, C, T, D, F = 16, 4, 128, 2048, 512
Q = 4
W = D // Q
MR = Q * C
RR = E * MR
R = E * C
NS = 2
CH = 32


def dot(a, b, dims=((1,), (0,)), precision=None):
    return lax.dot_general(a, b, (dims, ((), ())), preferred_element_type=F32, precision=precision)


def kernel(nz, picked_ref, gate_ref, tok_h, og_h, win_h, wout_h,
           lo_h, tg_h, gg_ref, gpi_ref,
           tok, og, win, wout, lo, tg,
           rows_s, rows_r, sc_s, sc_r, eo_s, eo_r, ir_s, ir_r, g_v,
           x_v, x_sib, xt, bp, perm, perm_t, a_hi, a_lo, a_one,
           cs, cr, ls, lr,
           ld_sem, st_sem, a2a_ss, a2a_rs, sib_ss, sib_rs, c_ss, c_rs, l_ss, l_rs):
    ns = nz // 4
    me = lax.axis_index("expert")
    dp = lax.axis_index("dp")
    z, h = dp // 2, dp % 2
    sib = z * 2 + (1 - h)

    def zdev(offset):
        return (me, lax.rem(z + offset + nz, nz) * 2 + h)

    loads = [pltpu.make_async_copy(s, d, ld_sem.at[i])
             for i, (s, d) in enumerate([(tok_h, tok), (og_h, og), (win_h, win), (wout_h, wout)])]
    for c in loads:
        c.start()

    barrier = pltpu.get_barrier_semaphore()

    def greet(k, _):
        pl.semaphore_signal(barrier, inc=1, device_id=(lax.rem(me + k, E), dp), device_id_type=MESH)
        return 0

    lax.fori_loop(1, E, greet, 0)
    pl.semaphore_signal(barrier, inc=1, device_id=(me, sib), device_id_type=MESH)
    for off in (1, -1, 2, -2):
        pl.semaphore_signal(barrier, inc=1, device_id=zdev(off), device_id_type=MESH)

    def iota(shape, dim):
        return lax.broadcasted_iota(jnp.int32, shape, dim)

    pickf = picked_ref[...].astype(F32)
    gatef = gate_ref[...]
    sel_e = ((iota((RR, E), 0) >> 4) == iota((RR, E), 1)).astype(F32)
    pk4 = dot(sel_e, pickf, precision=lax.Precision.HIGHEST)
    w4 = dot(sel_e, gatef, precision=lax.Precision.HIGHEST)
    is_c = (iota((RR, C), 0) & 3) == iota((RR, C), 1)
    pk = jnp.sum(jnp.where(is_c, pk4, 0.0), axis=1, keepdims=True)
    w = jnp.sum(jnp.where(is_c, w4, 0.0), axis=1, keepdims=True)
    tgt = pk.astype(jnp.int32) + ((iota((RR, 1), 0) >> 2) & 3) * T
    gather = (iota((RR, Q * T), 1) == tgt).astype(F32).astype(BF)
    diag = iota((RR, RR), 0) == iota((RR, RR), 1)
    tgt_row = jnp.sum(jnp.where(diag, tgt.astype(F32), 0.0), axis=0, keepdims=True).astype(jnp.int32)
    w_row = jnp.sum(jnp.where(diag, w, 0.0), axis=0, keepdims=True)

    def quarters(ref):
        return jnp.concatenate([ref[:, q * W:(q + 1) * W] for q in range(Q)], axis=0)

    def exchange(k, src, dst):
        def send(i, _):
            e = lax.rem(me + i, E)
            pltpu.make_async_remote_copy(
                src_ref=src.at[pl.ds(pl.multiple_of(e * MR, MR), MR)],
                dst_ref=dst.at[pl.ds(pl.multiple_of(me * MR, MR), MR)],
                send_sem=a2a_ss.at[k], recv_sem=a2a_rs.at[k],
                device_id=(e, dp), device_id_type=MESH).start()
            return 0
        lax.fori_loop(1, E, send, 0)
        own = pl.ds(pl.multiple_of(me * MR, MR), MR)
        dst[own, :] = src[own, :]

    def landed(k, dst):
        part = dst.at[pl.ds(0, (E - 1) * MR)]
        pltpu.make_async_copy(part, part, a2a_rs.at[k]).wait()

    def left(k, src):
        part = src.at[pl.ds(0, (E - 1) * MR)]
        pltpu.make_async_copy(part, part, a2a_ss.at[k]).wait()

    loads[0].wait()
    rows_s[...] = dot(gather, quarters(tok)).astype(BF)
    pl.semaphore_wait(barrier, E - 1 + 1 + 4)
    exchange(0, rows_s, rows_r)
    loads[1].wait()
    grad_rows = dot(gather, quarters(og))
    g_v[...] = grad_rows.astype(BF)
    sc_s[...] = (w * grad_rows).astype(BF)
    exchange(1, sc_s, sc_r)

    i0, i1 = iota((RR, RR), 0), iota((RR, RR), 1)
    to_q = ((i0 >> 2) & 15) * MR + (i0 >> 6) * C + (i0 & 3)
    perm[...] = (i1 == to_q).astype(F32).astype(BF)
    to_q_t = ((i1 >> 2) & 15) * MR + (i1 >> 6) * C + (i1 & 3)
    perm_t[...] = (i0 == to_q_t).astype(F32).astype(BF)
    hit = iota((Q * T, RR), 0) == tgt_row
    a_one[...] = hit.astype(F32).astype(BF)
    w_hi = w_row.astype(BF).astype(F32)
    a_hi[...] = jnp.where(hit, w_hi, 0.0).astype(BF)
    a_lo[...] = jnp.where(hit, w_row - w_hi, 0.0).astype(BF)

    landed(0, rows_r)
    x_v[...] = dot(perm[...], rows_r[...]).astype(BF)
    to_sib = pltpu.make_async_remote_copy(
        src_ref=x_v, dst_ref=x_sib, send_sem=sib_ss.at[0], recv_sem=sib_rs.at[0],
        device_id=(me, sib), device_id_type=MESH)
    to_sib.start()
    loads[2].wait()
    pre = jnp.zeros((R, F), F32)
    for q in range(Q):
        pre += dot(x_v[q * R:(q + 1) * R, :], win[q * W:(q + 1) * W, :])
    cdf = 0.5 * (1.0 + lax.erf(pre * (1.0 / math.sqrt(2.0))))
    density = jnp.exp(-0.5 * pre * pre) * (1.0 / math.sqrt(2.0 * math.pi))
    hidden = (pre * cdf).astype(BF)
    slope = cdf + pre * density
    landed(1, sc_r)
    scq = dot(perm[...], sc_r[...]).astype(BF)
    loads[3].wait()
    back = jnp.zeros((R, F), F32)
    for q in range(Q):
        back += dot(scq[q * R:(q + 1) * R, :], wout[:, q * W:(q + 1) * W], ((1,), (1,)))
    bp[0:R, :] = (back * slope).astype(BF)
    bp_sib = pltpu.make_async_remote_copy(
        src_ref=bp.at[pl.ds(0, R)], dst_ref=bp.at[pl.ds(R, R)], send_sem=sib_ss.at[1], recv_sem=sib_rs.at[1],
        device_id=(me, sib), device_id_type=MESH)
    bp_sib.start()

    to_sib.wait_recv()
    for q in range(Q):
        both = jnp.concatenate([x_v[q * R:(q + 1) * R, :], x_sib[q * R:(q + 1) * R, :]], axis=0)
        xt[q * W:(q + 1) * W, :] = both.T
    bp_sib.wait_recv()

    sub = F // NS

    def chunk(offset):
        t = lax.rem(z + offset + 2 * nz, nz)
        return xt[pl.ds(pl.multiple_of(t * (2 * CH) + h * CH, CH), CH), :]

    def chain(s, d, u):
        return pltpu.make_async_remote_copy(
            src_ref=cs.at[d, s, u], dst_ref=cr.at[d, s, u], send_sem=c_ss.at[d, s, u], recv_sem=c_rs.at[d, s, u],
            device_id=zdev(-2 if d else 2), device_id_type=MESH)

    def leaf(s, d, u):
        return pltpu.make_async_remote_copy(
            src_ref=ls.at[d, s, u], dst_ref=lr.at[d, s, u], send_sem=l_ss.at[d, s, u], recv_sem=l_rs.at[d, s, u],
            device_id=zdev(-1 if d else 1), device_id_type=MESH)

    half = nz // 2

    def send_leaves(s, d, own):
        for u in range(NS):
            ls[d, s, u] = own[:, u * sub:(u + 1) * sub].astype(BF)
            leaf(s, d, u).start()

    def first():
        own = dot(jnp.concatenate([chunk(half - 1), chunk(1 - half), chunk(half)], axis=0), bp[...])
        send_leaves(1, 0, own[0:CH])
        send_leaves(1, 1, own[CH:2 * CH])
        for u in range(NS):
            cs[0, 0, u] = own[2 * CH:, u * sub:(u + 1) * sub].astype(BF)
            chain(0, 0, u).start()

    def step(s, with_left_chain=True):
        own = dot(jnp.concatenate([chunk(half + 1 - 2 * (s + 1)), chunk(2 * (s + 1) - half - 1),
                                   chunk(half - 2 * s), chunk(2 * s - half)], axis=0), bp[...])
        send_leaves(s + 1, 0, own[0:CH])
        send_leaves(s + 1, 1, own[CH:2 * CH])
        for u in range(NS):
            for d in range(2):
                mine = own[(2 + d) * CH:(3 + d) * CH, u * sub:(u + 1) * sub]
                leaf(s, d, u).wait_recv()
                mine = mine + lr[d, s, u].astype(F32)
                if d == 0 or with_left_chain:
                    chain(s - 1, d, u).wait_recv()
                    mine = mine + cr[d, s - 1, u].astype(F32)
                cs[d, s, u] = mine.astype(BF)
                chain(s, d, u).start()

    def last():
        own = dot(chunk(0), bp[...])
        for u in range(NS):
            mine = own[:, u * sub:(u + 1) * sub]
            for d in range(2):
                leaf(ns, d, u).wait_recv()
                mine = mine + lr[d, ns, u].astype(F32)
                chain(ns - 1, d, u).wait_recv()
                mine = mine + cr[d, ns - 1, u].astype(F32)
            gpi_ref[:, u * sub:(u + 1) * sub] = mine

    first()

    eo = jnp.concatenate([dot(hidden, wout[:, q * W:(q + 1) * W]).astype(BF) for q in range(Q)], axis=0)
    eo_s[...] = dot(perm_t[...], eo).astype(BF)
    exchange(2, eo_s, eo_r)
    step(1, False)
    back_pre = bp[0:R, :]
    ir = jnp.concatenate(
        [dot(back_pre, win[q * W:(q + 1) * W, :], ((1,), (1,))).astype(BF) for q in range(Q)], axis=0)
    ir_s[...] = dot(perm_t[...], ir).astype(BF)
    exchange(3, ir_s, ir_r)
    step(2)
    landed(2, eo_r)
    prod = jnp.sum(g_v[...].astype(F32) * eo_r[...].astype(F32), axis=1, keepdims=True)
    sel_t = ((iota((E, RR), 1) >> 4) == iota((E, RR), 0)).astype(F32)
    gg_ref[...] = dot(sel_t, jnp.where(is_c, prod, 0.0), precision=lax.Precision.HIGHEST)
    step(3)
    for q in range(Q):
        lo[:, q * W:(q + 1) * W] = (dot(a_hi[q * T:(q + 1) * T, :], eo_r[...])
                                    + dot(a_lo[q * T:(q + 1) * T, :], eo_r[...])).astype(BF)
    st0 = pltpu.make_async_copy(lo, lo_h, st_sem.at[0])
    st0.start()
    step(4)
    landed(3, ir_r)
    for q in range(Q):
        tg[:, q * W:(q + 1) * W] = dot(a_one[q * T:(q + 1) * T, :], ir_r[...]).astype(BF)
    st1 = pltpu.make_async_copy(tg, tg_h, st_sem.at[1])
    st1.start()

    def loop(s, _):
        step(s)
        return 0

    lax.fori_loop(5, ns, loop, 0)
    last()

    st0.wait()
    st1.wait()
    to_sib.wait_send()
    bp_sib.wait_send()
    for k, buf in enumerate((rows_s, sc_s, eo_s, ir_s)):
        left(k, buf)

    def drain(s, _):
        for u in range(NS):
            for d in range(2):
                leaf(s, d, u).wait_send()

        @pl.when(s < ns)
        def _():
            for u in range(NS):
                for d in range(2):
                    chain(s, d, u).wait_send()
        return 0

    for u in range(NS):
        chain(0, 0, u).wait_send()
    lax.fori_loop(1, ns + 1, drain, 0)


def body(nz, tokens, out_grad, proj_in, proj_out, picked, gate_values):
    ns = nz // 4
    hbm = pl.BlockSpec(memory_space=pl.ANY)
    vmem = pl.BlockSpec(memory_space=pltpu.VMEM)
    buf = pltpu.VMEM((RR, W), BF)
    sub = F // NS
    red = pltpu.VMEM((2, ns + 1, NS, CH, sub), BF)
    dma = pltpu.SemaphoreType.DMA
    lo, tg, gg, gpi = pl.pallas_call(
        functools.partial(kernel, nz),
        out_shape=(
            jax.ShapeDtypeStruct((T, D), BF),
            jax.ShapeDtypeStruct((T, D), BF),
            jax.ShapeDtypeStruct((E, C), F32),
            jax.ShapeDtypeStruct((CH, F), F32),
        ),
        in_specs=[vmem, vmem, hbm, hbm, hbm, hbm],
        out_specs=(hbm, hbm, vmem, vmem),
        scratch_shapes=[
            pltpu.VMEM((T, D), BF), pltpu.VMEM((T, D), BF), pltpu.VMEM((D, F), BF), pltpu.VMEM((F, D), BF),
            pltpu.VMEM((T, D), BF), pltpu.VMEM((T, D), BF),
            buf, buf, buf, buf, buf, buf, buf, buf, buf,
            buf, buf, pltpu.VMEM((D, 2 * R), BF), pltpu.VMEM((2 * R, F), BF),
            pltpu.VMEM((RR, RR), BF), pltpu.VMEM((RR, RR), BF),
            pltpu.VMEM((Q * T, RR), BF), pltpu.VMEM((Q * T, RR), BF), pltpu.VMEM((Q * T, RR), BF),
            red, red, red, red,
            dma((4,)), dma((2,)), dma((4,)), dma((4,)), dma((2,)), dma((2,)),
            dma((2, ns + 1, NS)), dma((2, ns + 1, NS)), dma((2, ns + 1, NS)), dma((2, ns + 1, NS)),
        ],
        compiler_params=pltpu.CompilerParams(
            collective_id=0, has_side_effects=True, vmem_limit_bytes=40 * 1024 * 1024),
        name="moe_layer",
    )(picked[0], gate_values[0], tokens, out_grad, proj_in[0], proj_out[0])
    return lo, tg, gg[None], gpi[None]


def solution(mesh):
    return jax.shard_map(
        functools.partial(body, mesh.shape["dp"] // 2),
        mesh=mesh,
        in_specs=(
            P(("expert", "dp"), None),
            P(("expert", "dp"), None),
            P("expert", None, None),
            P("expert", None, None),
            P(("expert", "dp"), None, None),
            P(("expert", "dp"), None, None),
        ),
        out_specs=(
            P(("expert", "dp"), None),
            P(("expert", "dp"), None),
            P(("expert", "dp"), None, None),
            P("expert", "dp", None),
        ),
        check_vma=False,
    )
```

```python
import functools
import math

import jax
import jax.numpy as jnp
from jax import lax
from jax.experimental import pallas as pl
from jax.experimental.pallas import tpu as pltpu
from jax.sharding import PartitionSpec as P

MESH = pl.DeviceIdType.MESH
BF = jnp.bfloat16
NT = ((1,), (1,))
F32 = jnp.float32
HIGH = lax.Precision.HIGHEST
E, C, T, D, F = 16, 4, 128, 2048, 512
Q = 4
W = D // Q
MR = Q * C
RR = E * MR
R = E * C
K = 2 * R
CH = 64
NS = 2
SR = CH // NS
GAPS = ((2, 3, 4, 7), (2, 3, 4, 6))
LANE, EXPRESS, PER_CHIP = 2.3, 1.6, 0.64


def side_plan(gaps):
    stops = [sum(gaps)]
    for g in gaps:
        stops.append(stops[-1] - g)
    roles, ready = {}, {}
    for d in range(stops[0], -1, -1):
        lane = d + 1 <= stops[0] and d + 1 not in stops
        at = ready[d + 1] + LANE if lane else 0.0
        express = d in stops and d != stops[0]
        hop = 1
        if express:
            last = stops[stops.index(d) - 1]
            at = max(at, ready[last] + EXPRESS + PER_CHIP * (last - d))
        if d in stops and d > 0:
            hop = d - stops[stops.index(d) + 1]
        ready[d] = at
        roles[d] = (lane, last if express else None, hop, at)
    return roles


PLANS = tuple(side_plan(g) for g in GAPS)
ORDER = sorted(((PLANS[s][d][3], -d, s) for s in range(2) for d in PLANS[s] if d > 0))
OFFSETS = sorted({1} | set(GAPS[0]) | set(GAPS[1]))
SLOTS = max(sum(g) for g in GAPS) + 1


def dot(a, b, dims=((1,), (0,)), precision=None):
    return lax.dot_general(a, b, (dims, ((), ())), preferred_element_type=F32, precision=precision)


def iota(shape, dim):
    return lax.broadcasted_iota(jnp.int32, shape, dim)


def kernel(nz, picked_h, gate_h, tok_h, og_h, win_h, wout_h,
           lo, tg, gg, gpi_o,
           picked, gate, tok, og, win, wout, gpi,
           rows_s, sc_s, rows_r, sc_r, eo_s, ir_s, eo_r, ir_r, g_v,
           x_v, xt, hid, bp, perm, perm_t, a_hi, a_lo, a_one, ms, mr,
           ld_sem, in_ss, in_rs, out_ss, out_rs, sib_ss, sib_rs, m_ss, m_rs):
    me = lax.axis_index("expert")
    dp = lax.axis_index("dp")
    z, h = dp // 2, dp % 2
    even, odd = z * 2, z * 2 + 1

    def zdev(offset):
        return (me, lax.rem(z + offset + nz, nz) * 2 + h)

    barrier = pltpu.get_barrier_semaphore()

    def signal(dev):
        pl.semaphore_signal(barrier, inc=1, device_id=dev, device_id_type=MESH)

    def greet(k, _):
        e = lax.rem(me + k, E)
        signal((e, odd))
        signal((e, even))
        return 0

    lax.fori_loop(1, E, greet, 0)
    signal((me, z * 2 + (1 - h)))

    @pl.when(h == 1)
    def _():
        for off in OFFSETS:
            signal(zdev(off))
            signal(zdev(-off))

    pairs = [(picked_h, picked), (gate_h, gate), (tok_h, tok), (og_h, og), (win_h, win), (wout_h, wout)]
    loads = [pltpu.make_async_copy(s, d, ld_sem.at[i]) for i, (s, d) in enumerate(pairs)]
    for c in loads:
        c.start()

    sel_e = ((iota((RR, E), 0) >> 4) == iota((RR, E), 1)).astype(F32)
    is_c = (iota((RR, C), 0) & 3) == iota((RR, C), 1)
    diag = iota((RR, RR), 0) == iota((RR, RR), 1)
    loads[0].wait()
    loads[1].wait()
    pk4 = dot(sel_e, picked[...].astype(F32), NT, HIGH)
    w4 = dot(sel_e, gate[...], NT, HIGH)
    pk = jnp.sum(jnp.where(is_c, pk4, 0.0), axis=1, keepdims=True)
    w = jnp.sum(jnp.where(is_c, w4, 0.0), axis=1, keepdims=True)
    tgt = pk.astype(jnp.int32) + ((iota((RR, 1), 0) >> 2) & 3) * T
    gather = (iota((RR, Q * T), 1) == tgt).astype(F32).astype(BF)

    def quarters(ref):
        return jnp.concatenate([ref[:, q * W:(q + 1) * W] for q in range(Q)], axis=0)

    def block(i, base=0):
        return pl.ds(pl.multiple_of(base + i * MR, MR), MR)

    def send_in(k, src, dst):
        def copy(e):
            return pltpu.make_async_remote_copy(
                src_ref=src.at[block(e)], dst_ref=dst.at[block(me, h * RR)],
                send_sem=in_ss.at[k], recv_sem=in_rs.at[k, h],
                device_id=(e, odd), device_id_type=MESH)

        def send(i, _):
            copy(lax.rem(me + i, E)).start()
            return 0

        lax.fori_loop(1, E, send, 0)

        @pl.when(h == 0)
        def _():
            copy(me).start()

        @pl.when(h == 1)
        def _():
            dst[block(me, RR), :] = src[block(me), :]

    def wait_rows(ref, start, count, sem):
        part = ref.at[pl.ds(start, count)]
        pltpu.make_async_copy(part, part, sem).wait()

    loads[2].wait()
    rows_s[...] = dot(gather, quarters(tok)).astype(BF)

    @pl.when(h == 0)
    def _():
        pl.semaphore_wait(barrier, 2 * E - 1)

    @pl.when(h == 1)
    def _():
        pl.semaphore_wait(barrier, 2 * E - 1 + 2 * len(OFFSETS))

    send_in(0, rows_s, rows_r)
    loads[3].wait()
    grad_rows = dot(gather, quarters(og))
    sc_s[...] = (w * grad_rows).astype(BF)
    send_in(1, sc_s, sc_r)
    g_v[...] = grad_rows.astype(BF)

    i0, i1 = iota((RR, RR), 0), iota((RR, RR), 1)
    to_q = ((i0 >> 2) & 15) * MR + (i0 >> 6) * C + (i0 & 3)
    perm[...] = (i1 == to_q).astype(F32).astype(BF)
    to_q_t = ((i1 >> 2) & 15) * MR + (i1 >> 6) * C + (i1 & 3)
    perm_t[...] = (i0 == to_q_t).astype(F32).astype(BF)
    tgt_row = jnp.sum(jnp.where(diag, tgt.astype(F32), 0.0), axis=0, keepdims=True).astype(jnp.int32)
    w_row = jnp.sum(jnp.where(diag, w, 0.0), axis=0, keepdims=True)
    hit = iota((Q * T, RR), 0) == tgt_row
    a_one[...] = hit.astype(F32).astype(BF)
    w_hi = w_row.astype(BF).astype(F32)
    a_hi[...] = jnp.where(hit, w_hi, 0.0).astype(BF)
    a_lo[...] = jnp.where(hit, w_row - w_hi, 0.0).astype(BF)

    def combine_out():
        for q in range(Q):
            a = slice(q * T, (q + 1) * T)
            lo[:, q * W:(q + 1) * W] = (dot(a_hi[a, :], eo_r[...]) + dot(a_lo[a, :], eo_r[...])).astype(BF)
        prod = jnp.sum(g_v[...].astype(F32) * eo_r[...].astype(F32), axis=1, keepdims=True)
        sel_t = ((iota((E, RR), 1) >> 4) == iota((E, RR), 0)).astype(F32)
        prod_row = jnp.sum(jnp.where(diag, prod, 0.0), axis=0, keepdims=True)
        by_c = jnp.where((iota((C, RR), 1) & 3) == iota((C, RR), 0), prod_row, 0.0)
        gg[...] = dot(by_c, sel_t, NT, HIGH)

    def combine_grad():
        for q in range(Q):
            tg[:, q * W:(q + 1) * W] = dot(a_one[q * T:(q + 1) * T, :], ir_r[...]).astype(BF)

    def to_sib(i, src, dst):
        return pltpu.make_async_remote_copy(
            src_ref=src, dst_ref=dst, send_sem=sib_ss.at[i], recv_sem=sib_rs.at[i],
            device_id=(me, z * 2 + (1 - h)), device_id_type=MESH)

    hid_copy = to_sib(0, hid, hid)
    bp_copy = to_sib(1, bp, bp)
    gpi_copy = to_sib(2, gpi, gpi_o)

    def by_quarter(src, dst):
        for cs in range(2):
            xs = dot(perm[...], src[cs * RR:(cs + 1) * RR, :]).astype(BF)
            for q in range(Q):
                dst[q, cs * R:(cs + 1) * R, :] = xs[q * R:(q + 1) * R, :]

    @pl.when(h == 1)
    def _():
        wait_rows(rows_r, 0, RR, in_rs.at[0, 0])
        wait_rows(rows_r, RR, RR - MR, in_rs.at[0, 1])
        by_quarter(rows_r, x_v)
        loads[4].wait()
        pre = dot(x_v[0], win[0:W, :])
        for q in range(1, Q):
            pre += dot(x_v[q], win[q * W:(q + 1) * W, :])
        cdf = 0.5 * (1.0 + lax.erf(pre * (1.0 / math.sqrt(2.0))))
        hid[...] = (pre * cdf).astype(BF)
        hid_copy.start()
        slope = cdf + pre * (jnp.exp(-0.5 * pre * pre) * (1.0 / math.sqrt(2.0 * math.pi)))
        for q in range(Q):
            xt[q * W:(q + 1) * W, :] = x_v[q].T
        loads[5].wait()
        wait_rows(sc_r, 0, RR, in_rs.at[1, 0])
        wait_rows(sc_r, RR, RR - MR, in_rs.at[1, 1])
        by_quarter(sc_r, x_v)
        back = dot(x_v[0], wout[:, 0:W], NT)
        for q in range(1, Q):
            back += dot(x_v[q], wout[:, q * W:(q + 1) * W], NT)
        bp[...] = (back * slope).astype(BF)
        bp_copy.start()

        def own(s, d):
            t = lax.rem(z + (d if s == 0 else -d) + nz, nz)
            return dot(xt[pl.ds(pl.multiple_of(t * CH, CH), CH), :], bp[...])

        def message(s, d, u):
            hop = PLANS[s][d][2]
            part = pl.ds(u * SR, SR)
            return pltpu.make_async_remote_copy(
                src_ref=ms.at[s, d, part], dst_ref=mr.at[s, d, part],
                send_sem=m_ss.at[s, d, u], recv_sem=m_rs.at[s, d, u],
                device_id=zdev(hop if s == 0 else -hop), device_id_type=MESH)

        def add(total, s, d, u):
            message(s, d, u).wait_recv()
            return total + mr[s, d, u * SR:(u + 1) * SR, :].astype(F32)

        def gathered(total, s, d, u):
            lane, last, _, _ = PLANS[s][d]
            if lane:
                total = add(total, s, d + 1, u)
            if last is not None:
                total = add(total, s, last, u)
            return total

        def role(s, d):
            mine = own(s, d)
            for u in range(NS):
                total = gathered(mine[u * SR:(u + 1) * SR], s, d, u)
                ms[s, d, u * SR:(u + 1) * SR, :] = total.astype(BF)
                message(s, d, u).start()

        for _, nd, s in ORDER:
            role(s, -nd)

        wait_rows(eo_r, 0, RR, out_rs.at[0])
        combine_out()
        wait_rows(ir_r, 0, RR, out_rs.at[1])
        combine_grad()

        mine = own(0, 0)
        for u in range(NS):
            total = mine[u * SR:(u + 1) * SR]
            for s in range(2):
                total = gathered(total, s, 0, u)
            for i in range(u * SR, (u + 1) * SR, min(SR, CH // 2)):
                part = total[i - u * SR:i - u * SR + min(SR, CH // 2)]
                if i < CH // 2:
                    gpi[i:i + part.shape[0], :] = part
                else:
                    gpi_o[i - CH // 2:i - CH // 2 + part.shape[0], :] = part
            if (u + 1) * SR == max(SR, CH // 2):
                gpi_copy.start()
        wait_rows(rows_s, 0, RR - MR, in_ss.at[0])
        wait_rows(sc_s, 0, RR - MR, in_ss.at[1])
        hid_copy.wait_send()
        bp_copy.wait_send()
        for s in range(2):
            for d in PLANS[s]:
                if d > 0:
                    for u in range(NS):
                        message(s, d, u).wait_send()
        gpi_copy.wait_send()

    @pl.when(h == 0)
    def _():
        def send_out(k, src, dst):
            def copy(cs, e):
                return pltpu.make_async_remote_copy(
                    src_ref=src.at[block(e, cs * RR)], dst_ref=dst.at[block(me)],
                    send_sem=out_ss.at[k, cs], recv_sem=out_rs.at[k],
                    device_id=(e, z * 2 + cs), device_id_type=MESH)

            def send(i, _):
                e = lax.rem(me + i, E)
                copy(1, e).start()
                copy(0, e).start()
                return 0

            lax.fori_loop(1, E, send, 0)
            copy(1, me).start()
            dst[block(me), :] = src[block(me), :]

        def by_source(parts, dst):
            for cs in range(2):
                rows = jnp.concatenate([p[cs * R:(cs + 1) * R] for p in parts], axis=0)
                dst[cs * RR:(cs + 1) * RR, :] = dot(perm_t[...], rows).astype(BF)

        loads[4].wait()
        loads[5].wait()
        hid_copy.wait_recv()
        by_source([dot(hid[...], wout[:, q * W:(q + 1) * W]).astype(BF) for q in range(Q)], eo_s)
        send_out(0, eo_s, eo_r)
        bp_copy.wait_recv()
        by_source([dot(bp[...], win[q * W:(q + 1) * W, :], NT).astype(BF) for q in range(Q)], ir_s)
        send_out(1, ir_s, ir_r)
        wait_rows(eo_r, 0, RR - MR, out_rs.at[0])
        combine_out()
        wait_rows(ir_r, 0, RR - MR, out_rs.at[1])
        combine_grad()
        wait_rows(rows_s, 0, RR, in_ss.at[0])
        wait_rows(sc_s, 0, RR, in_ss.at[1])
        for k, src in enumerate((eo_s, ir_s)):
            wait_rows(src, 0, RR - MR, out_ss.at[k, 0])
            wait_rows(src, 0, RR, out_ss.at[k, 1])
        gpi_copy.wait_recv()


def copy_out(a, b, c, d, oa, ob, oc, od, sem):
    copies = [pltpu.make_async_copy(s, t, sem.at[i]) for i, (s, t) in enumerate(((a, oa), (b, ob), (c, oc), (d, od)))]
    for x in copies:
        x.start()
    for x in copies:
        x.wait()


def body(nz, tokens, out_grad, proj_in, proj_out, picked, gate_values):
    hbm = pl.BlockSpec(memory_space=pltpu.HBM)
    vmem = pl.BlockSpec(memory_space=pltpu.VMEM)
    dma = pltpu.SemaphoreType.DMA

    def buf(*shape, dtype=BF):
        return pltpu.VMEM(shape, dtype)

    shapes = (
        jax.ShapeDtypeStruct((T, D), BF),
        jax.ShapeDtypeStruct((T, D), BF),
        jax.ShapeDtypeStruct((C, E), F32),
        jax.ShapeDtypeStruct((CH // 2, F), F32),
    )
    outs = pl.pallas_call(
        functools.partial(kernel, nz),
        out_shape=shapes,
        in_specs=[hbm] * 6,
        out_specs=(vmem,) * 4,
        scratch_shapes=[
            buf(C, E, dtype=jnp.int32), buf(C, E, dtype=F32), buf(T, D), buf(T, D), buf(D, F), buf(F, D),
            buf(CH // 2, F, dtype=F32),
            buf(RR, W), buf(RR, W), buf(2 * RR, W), buf(2 * RR, W), buf(2 * RR, W), buf(2 * RR, W),
            buf(RR, W), buf(RR, W), buf(RR, W),
            buf(Q, K, W), buf(D, K), buf(K, F), buf(K, F), buf(RR, RR), buf(RR, RR),
            buf(Q * T, RR), buf(Q * T, RR), buf(Q * T, RR),
            buf(2, SLOTS, CH, F), buf(2, SLOTS, CH, F),
            dma((6,)), dma((2,)), dma((2, 2)), dma((2, 2)), dma((2,)), dma((3,)), dma((3,)),
            dma((2, SLOTS, NS)), dma((2, SLOTS, NS)),
        ],
        compiler_params=pltpu.CompilerParams(
            collective_id=0, has_side_effects=True, vmem_limit_bytes=60 * 1024 * 1024),
        name="moe_layer",
    )(picked[0].T, gate_values[0].T, tokens, out_grad, proj_in[0], proj_out[0])
    lo, tg, gg, gpi = pl.pallas_call(
        copy_out, out_shape=shapes, in_specs=[vmem] * 4, out_specs=(hbm,) * 4,
        scratch_shapes=[dma((4,))], name="copy_out",
    )(*outs)
    return lo, tg, gg.T[None], gpi[None]


def solution(mesh):
    return jax.shard_map(
        functools.partial(body, mesh.shape["dp"] // 2),
        mesh=mesh,
        in_specs=(
            P(("expert", "dp"), None),
            P(("expert", "dp"), None),
            P("expert", None, None),
            P("expert", None, None),
            P(("expert", "dp"), None, None),
            P(("expert", "dp"), None, None),
        ),
        out_specs=(
            P(("expert", "dp"), None),
            P(("expert", "dp"), None),
            P(("expert", "dp"), None, None),
            P("expert", "dp", None),
        ),
        check_vma=False,
    )
```

```python
import functools
import math

import jax
import jax.numpy as jnp
from jax import lax
from jax.experimental import pallas as pl
from jax.experimental.pallas import tpu as pltpu
from jax.sharding import PartitionSpec as P

MESH = pl.DeviceIdType.MESH
BF = jnp.bfloat16
NT = ((1,), (1,))
F32 = jnp.float32
HIGH = lax.Precision.HIGHEST
E, C, T, D, F = 16, 4, 128, 2048, 512
Q = 4
W = D // Q
MR = Q * C
RR = E * MR
R = E * C
K = 2 * R
CH = 64
NS = 2
SR = CH // NS
GAPS = ((2, 3, 3, 4, 4), (2, 3, 3, 4, 3))
STOPS = tuple(tuple(sum(g[i:]) for i in range(len(g) + 1)) for g in GAPS)
BETWEEN = tuple([(i, j) for i in range(1, len(g) + 1) for j in range(1, g[i - 1])] for g in GAPS)
REACH = max(max(g) for g in GAPS) - 1
OFFSETS = sorted(set(range(1, REACH + 1)) | set(GAPS[0]) | set(GAPS[1]))
SLICES = max(len(b) for b in BETWEEN)
STEPS = max(len(g) for g in GAPS)


def dot(a, b, dims=((1,), (0,)), precision=None):
    return lax.dot_general(a, b, (dims, ((), ())), preferred_element_type=F32, precision=precision)


def iota(shape, dim):
    return lax.broadcasted_iota(jnp.int32, shape, dim)


def kernel(nz, picked_h, gate_h, tok_h, og_h, win_h, wout_h,
           lo, tg, gg, gpi_o,
           picked, gate, tok, og, win, wout, gpi,
           rows_s, sc_s, rows_r, sc_r, eo_s, ir_s, eo_r, ir_r, g_v,
           x_v, xt, hid, bp, perm, perm_t, a_hi, a_lo, a_one, xs, bpn, ms, mr,
           ld_sem, in_ss, in_rs, out_ss, out_rs, sib_ss, sib_rs, m_ss, m_rs, x_ss, x_rs, b_ss, b_rs):
    me = lax.axis_index("expert")
    dp = lax.axis_index("dp")
    z, h = dp // 2, dp % 2
    even, odd = z * 2, z * 2 + 1

    def zdev(offset):
        return (me, lax.rem(z + offset + nz, nz) * 2 + h)

    barrier = pltpu.get_barrier_semaphore()

    def signal(dev):
        pl.semaphore_signal(barrier, inc=1, device_id=dev, device_id_type=MESH)

    def greet(k, _):
        e = lax.rem(me + k, E)
        signal((e, odd))
        signal((e, even))
        return 0

    lax.fori_loop(1, E, greet, 0)
    signal((me, z * 2 + (1 - h)))

    @pl.when(h == 1)
    def _():
        for off in OFFSETS:
            signal(zdev(off))
            signal(zdev(-off))

    pairs = [(picked_h, picked), (gate_h, gate), (tok_h, tok), (og_h, og), (win_h, win), (wout_h, wout)]
    loads = [pltpu.make_async_copy(s, d, ld_sem.at[i]) for i, (s, d) in enumerate(pairs)]
    for c in loads:
        c.start()

    sel_e = ((iota((RR, E), 0) >> 4) == iota((RR, E), 1)).astype(F32)
    is_c = (iota((RR, C), 0) & 3) == iota((RR, C), 1)
    diag = iota((RR, RR), 0) == iota((RR, RR), 1)
    loads[0].wait()
    loads[1].wait()
    pk4 = dot(sel_e, picked[...].astype(F32), NT, HIGH)
    w4 = dot(sel_e, gate[...], NT, HIGH)
    pk = jnp.sum(jnp.where(is_c, pk4, 0.0), axis=1, keepdims=True)
    w = jnp.sum(jnp.where(is_c, w4, 0.0), axis=1, keepdims=True)
    tgt = pk.astype(jnp.int32) + ((iota((RR, 1), 0) >> 2) & 3) * T
    gather = (iota((RR, Q * T), 1) == tgt).astype(F32).astype(BF)

    def quarters(ref):
        return jnp.concatenate([ref[:, q * W:(q + 1) * W] for q in range(Q)], axis=0)

    def block(i, base=0):
        return pl.ds(pl.multiple_of(base + i * MR, MR), MR)

    def send_in(k, src, dst):
        def copy(e):
            return pltpu.make_async_remote_copy(
                src_ref=src.at[block(e)], dst_ref=dst.at[block(me, h * RR)],
                send_sem=in_ss.at[k], recv_sem=in_rs.at[k, h],
                device_id=(e, odd), device_id_type=MESH)

        def send(i, _):
            copy(lax.rem(me + i, E)).start()
            return 0

        lax.fori_loop(1, E, send, 0)

        @pl.when(h == 0)
        def _():
            copy(me).start()

        @pl.when(h == 1)
        def _():
            dst[block(me, RR), :] = src[block(me), :]

    def wait_rows(ref, start, count, sem):
        part = ref.at[pl.ds(start, count)]
        pltpu.make_async_copy(part, part, sem).wait()

    loads[2].wait()
    rows_s[...] = dot(gather, quarters(tok)).astype(BF)

    @pl.when(h == 0)
    def _():
        pl.semaphore_wait(barrier, 2 * E - 1)

    @pl.when(h == 1)
    def _():
        pl.semaphore_wait(barrier, 2 * E - 1 + 2 * len(OFFSETS))

    send_in(0, rows_s, rows_r)
    loads[3].wait()
    grad_rows = dot(gather, quarters(og))
    sc_s[...] = (w * grad_rows).astype(BF)
    send_in(1, sc_s, sc_r)
    g_v[...] = grad_rows.astype(BF)

    i0, i1 = iota((RR, RR), 0), iota((RR, RR), 1)
    to_q = ((i0 >> 2) & 15) * MR + (i0 >> 6) * C + (i0 & 3)
    perm[...] = (i1 == to_q).astype(F32).astype(BF)
    to_q_t = ((i1 >> 2) & 15) * MR + (i1 >> 6) * C + (i1 & 3)
    perm_t[...] = (i0 == to_q_t).astype(F32).astype(BF)
    tgt_row = jnp.sum(jnp.where(diag, tgt.astype(F32), 0.0), axis=0, keepdims=True).astype(jnp.int32)
    w_row = jnp.sum(jnp.where(diag, w, 0.0), axis=0, keepdims=True)
    hit = iota((Q * T, RR), 0) == tgt_row
    a_one[...] = hit.astype(F32).astype(BF)
    w_hi = w_row.astype(BF).astype(F32)
    a_hi[...] = jnp.where(hit, w_hi, 0.0).astype(BF)
    a_lo[...] = jnp.where(hit, w_row - w_hi, 0.0).astype(BF)

    def combine_out():
        for q in range(Q):
            a = slice(q * T, (q + 1) * T)
            lo[:, q * W:(q + 1) * W] = (dot(a_hi[a, :], eo_r[...]) + dot(a_lo[a, :], eo_r[...])).astype(BF)
        prod = jnp.sum(g_v[...].astype(F32) * eo_r[...].astype(F32), axis=1, keepdims=True)
        sel_t = ((iota((E, RR), 1) >> 4) == iota((E, RR), 0)).astype(F32)
        prod_row = jnp.sum(jnp.where(diag, prod, 0.0), axis=0, keepdims=True)
        by_c = jnp.where((iota((C, RR), 1) & 3) == iota((C, RR), 0), prod_row, 0.0)
        gg[...] = dot(by_c, sel_t, NT, HIGH)

    def combine_grad():
        for q in range(Q):
            tg[:, q * W:(q + 1) * W] = dot(a_one[q * T:(q + 1) * T, :], ir_r[...]).astype(BF)

    def to_sib(i, src, dst):
        return pltpu.make_async_remote_copy(
            src_ref=src, dst_ref=dst, send_sem=sib_ss.at[i], recv_sem=sib_rs.at[i],
            device_id=(me, z * 2 + (1 - h)), device_id_type=MESH)

    hid_copy = to_sib(0, hid, hid)
    bp_copy = to_sib(1, bp, bp)
    gpi_copy = to_sib(2, gpi, gpi_o)

    def by_quarter(src, dst):
        for cs in range(2):
            xs = dot(perm[...], src[cs * RR:(cs + 1) * RR, :]).astype(BF)
            for q in range(Q):
                dst[q, cs * R:(cs + 1) * R, :] = xs[q * R:(q + 1) * R, :]

    def along(s, hops):
        return zdev(hops if s == 0 else -hops)

    def columns(s, d):
        t = lax.rem(z + (d if s == 0 else -d) + nz, nz)
        return pl.ds(pl.multiple_of(t * CH, CH), CH)

    @pl.when(h == 1)
    def _():
        wait_rows(rows_r, 0, RR, in_rs.at[0, 0])
        wait_rows(rows_r, RR, RR - MR, in_rs.at[0, 1])
        by_quarter(rows_r, x_v)
        loads[4].wait()
        pre = dot(x_v[0], win[0:W, :])
        for q in range(1, Q):
            pre += dot(x_v[q], win[q * W:(q + 1) * W, :])
        cdf = 0.5 * (1.0 + lax.erf(pre * (1.0 / math.sqrt(2.0))))
        hid[...] = (pre * cdf).astype(BF)
        hid_copy.start()
        slope = cdf + pre * (jnp.exp(-0.5 * pre * pre) * (1.0 / math.sqrt(2.0 * math.pi)))
        for q in range(Q):
            xt[q * W:(q + 1) * W, :] = x_v[q].T
        for s in range(2):
            for n, (i, j) in enumerate(BETWEEN[s]):
                pltpu.make_async_remote_copy(
                    src_ref=xt.at[columns(s, STOPS[s][i] + j)], dst_ref=xs.at[s, pl.ds(n * CH, CH)],
                    send_sem=x_ss.at[s], recv_sem=x_rs.at[s], device_id=along(s, j), device_id_type=MESH).start()
        loads[5].wait()
        wait_rows(sc_r, 0, RR, in_rs.at[1, 0])
        wait_rows(sc_r, RR, RR - MR, in_rs.at[1, 1])
        by_quarter(sc_r, x_v)
        back = dot(x_v[0], wout[:, 0:W], NT)
        for q in range(1, Q):
            back += dot(x_v[q], wout[:, q * W:(q + 1) * W], NT)
        bp[...] = (back * slope).astype(BF)
        bp_copy.start()

        def pass_on(s, j):
            return pltpu.make_async_remote_copy(
                src_ref=bpn.at[s, j - 1] if j else bp, dst_ref=bpn.at[s, j],
                send_sem=b_ss.at[s, j], recv_sem=b_rs.at[s, j], device_id=along(s, 1), device_id_type=MESH)

        def message(s, i, u):
            part = pl.ds(u * SR, SR)
            return pltpu.make_async_remote_copy(
                src_ref=ms.at[s, i, part], dst_ref=mr.at[s, i, part],
                send_sem=m_ss.at[s, i, u], recv_sem=m_rs.at[s, i, u],
                device_id=along(s, GAPS[s][i]), device_id_type=MESH)

        arrived = [0]

        def need(j):
            while arrived[0] < j:
                k = arrived[0]
                for s in range(2):
                    pass_on(s, k).wait_recv()
                    if k + 1 < REACH:
                        pass_on(s, k + 1).start()
                arrived[0] += 1

        def others(s, i):
            total = None
            for n, (k, j) in enumerate(BETWEEN[s]):
                if k == i:
                    need(j)
                    term = dot(xs[s, n * CH:(n + 1) * CH, :], bpn[s, j - 1])
                    total = term if total is None else total + term
            return total

        def add(total, s, i, u):
            message(s, i - 1, u).wait_recv()
            return total + mr[s, i - 1, u * SR:(u + 1) * SR, :].astype(F32)

        def stop(s, i):
            mine = dot(xt[columns(s, STOPS[s][i]), :], bp[...])
            if i:
                mine = mine + others(s, i)
            for u in range(NS):
                total = mine[u * SR:(u + 1) * SR]
                if i:
                    total = add(total, s, i, u)
                ms[s, i, u * SR:(u + 1) * SR, :] = total.astype(BF)
                message(s, i, u).start()

        for s in range(2):
            pass_on(s, 0).start()
        for s in range(2):
            stop(s, 0)
        for s in range(2):
            wait_rows(xs.at[s], 0, len(BETWEEN[s]) * CH, x_rs.at[s])
        for i in range(1, STEPS):
            for s in range(2):
                stop(s, i)
            if i == STEPS - 2:
                wait_rows(eo_r, 0, RR, out_rs.at[0])
                combine_out()
        wait_rows(ir_r, 0, RR, out_rs.at[1])
        combine_grad()

        mine = dot(xt[columns(0, 0), :], bp[...]) + others(0, STEPS) + others(1, STEPS)
        need(REACH)
        for u in range(NS):
            total = mine[u * SR:(u + 1) * SR]
            for s in range(2):
                total = add(total, s, STEPS, u)
            for i in range(u * SR, (u + 1) * SR, min(SR, CH // 2)):
                part = total[i - u * SR:i - u * SR + min(SR, CH // 2)]
                if i < CH // 2:
                    gpi[i:i + part.shape[0], :] = part
                else:
                    gpi_o[i - CH // 2:i - CH // 2 + part.shape[0], :] = part
            if (u + 1) * SR == max(SR, CH // 2):
                gpi_copy.start()
        wait_rows(rows_s, 0, RR - MR, in_ss.at[0])
        wait_rows(sc_s, 0, RR - MR, in_ss.at[1])
        hid_copy.wait_send()
        bp_copy.wait_send()
        for s in range(2):
            wait_rows(xs.at[s], 0, len(BETWEEN[s]) * CH, x_ss.at[s])
            for j in range(REACH):
                pass_on(s, j).wait_send()
            for i in range(STEPS):
                for u in range(NS):
                    message(s, i, u).wait_send()
        gpi_copy.wait_send()

    @pl.when(h == 0)
    def _():
        def send_out(k, src, dst):
            def copy(cs, e):
                return pltpu.make_async_remote_copy(
                    src_ref=src.at[block(e, cs * RR)], dst_ref=dst.at[block(me)],
                    send_sem=out_ss.at[k, cs], recv_sem=out_rs.at[k],
                    device_id=(e, z * 2 + cs), device_id_type=MESH)

            def send(i, _):
                e = lax.rem(me + i, E)
                copy(1, e).start()
                copy(0, e).start()
                return 0

            lax.fori_loop(1, E, send, 0)
            copy(1, me).start()
            dst[block(me), :] = src[block(me), :]

        def by_source(parts, dst):
            for cs in range(2):
                rows = jnp.concatenate([p[cs * R:(cs + 1) * R] for p in parts], axis=0)
                dst[cs * RR:(cs + 1) * RR, :] = dot(perm_t[...], rows).astype(BF)

        loads[4].wait()
        loads[5].wait()
        hid_copy.wait_recv()
        by_source([dot(hid[...], wout[:, q * W:(q + 1) * W]).astype(BF) for q in range(Q)], eo_s)
        send_out(0, eo_s, eo_r)
        bp_copy.wait_recv()
        by_source([dot(bp[...], win[q * W:(q + 1) * W, :], NT).astype(BF) for q in range(Q)], ir_s)
        send_out(1, ir_s, ir_r)
        wait_rows(eo_r, 0, RR - MR, out_rs.at[0])
        combine_out()
        wait_rows(ir_r, 0, RR - MR, out_rs.at[1])
        combine_grad()
        wait_rows(rows_s, 0, RR, in_ss.at[0])
        wait_rows(sc_s, 0, RR, in_ss.at[1])
        for k, src in enumerate((eo_s, ir_s)):
            wait_rows(src, 0, RR - MR, out_ss.at[k, 0])
            wait_rows(src, 0, RR, out_ss.at[k, 1])
        gpi_copy.wait_recv()


def copy_out(a, b, c, d, oa, ob, oc, od, sem):
    copies = [pltpu.make_async_copy(s, t, sem.at[i]) for i, (s, t) in enumerate(((a, oa), (b, ob), (c, oc), (d, od)))]
    for x in copies:
        x.start()
    for x in copies:
        x.wait()


def body(nz, tokens, out_grad, proj_in, proj_out, picked, gate_values):
    hbm = pl.BlockSpec(memory_space=pltpu.HBM)
    vmem = pl.BlockSpec(memory_space=pltpu.VMEM)
    dma = pltpu.SemaphoreType.DMA

    def buf(*shape, dtype=BF):
        return pltpu.VMEM(shape, dtype)

    shapes = (
        jax.ShapeDtypeStruct((T, D), BF),
        jax.ShapeDtypeStruct((T, D), BF),
        jax.ShapeDtypeStruct((C, E), F32),
        jax.ShapeDtypeStruct((CH // 2, F), F32),
    )
    outs = pl.pallas_call(
        functools.partial(kernel, nz),
        out_shape=shapes,
        in_specs=[hbm] * 6,
        out_specs=(vmem,) * 4,
        scratch_shapes=[
            buf(C, E, dtype=jnp.int32), buf(C, E, dtype=F32), buf(T, D), buf(T, D), buf(D, F), buf(F, D),
            buf(CH // 2, F, dtype=F32),
            buf(RR, W), buf(RR, W), buf(2 * RR, W), buf(2 * RR, W), buf(2 * RR, W), buf(2 * RR, W),
            buf(RR, W), buf(RR, W), buf(RR, W),
            buf(Q, K, W), buf(D, K), buf(K, F), buf(K, F), buf(RR, RR), buf(RR, RR),
            buf(Q * T, RR), buf(Q * T, RR), buf(Q * T, RR),
            buf(2, SLICES * CH, K), buf(2, REACH, K, F), buf(2, STEPS, CH, F), buf(2, STEPS, CH, F),
            dma((6,)), dma((2,)), dma((2, 2)), dma((2, 2)), dma((2,)), dma((3,)), dma((3,)),
            dma((2, STEPS, NS)), dma((2, STEPS, NS)), dma((2,)), dma((2,)), dma((2, REACH)), dma((2, REACH)),
        ],
        compiler_params=pltpu.CompilerParams(
            collective_id=0, has_side_effects=True, vmem_limit_bytes=60 * 1024 * 1024),
        name="moe_layer",
    )(picked[0].T, gate_values[0].T, tokens, out_grad, proj_in[0], proj_out[0])
    lo, tg, gg, gpi = pl.pallas_call(
        copy_out, out_shape=shapes, in_specs=[vmem] * 4, out_specs=(hbm,) * 4,
        scratch_shapes=[dma((4,))], name="copy_out",
    )(*outs)
    return lo, tg, gg.T[None], gpi[None]


def solution(mesh):
    return jax.shard_map(
        functools.partial(body, mesh.shape["dp"] // 2),
        mesh=mesh,
        in_specs=(
            P(("expert", "dp"), None),
            P(("expert", "dp"), None),
            P("expert", None, None),
            P("expert", None, None),
            P(("expert", "dp"), None, None),
            P(("expert", "dp"), None, None),
        ),
        out_specs=(
            P(("expert", "dp"), None),
            P(("expert", "dp"), None),
            P(("expert", "dp"), None, None),
            P("expert", "dp", None),
        ),
        check_vma=False,
    )
```

```python
import functools
import math

import jax
import jax.numpy as jnp
from jax import lax
from jax.experimental import pallas as pl
from jax.experimental.pallas import tpu as pltpu
from jax.sharding import PartitionSpec as P

MESH = pl.DeviceIdType.MESH
BF = jnp.bfloat16
NT = ((1,), (1,))
F32 = jnp.float32
HIGH = lax.Precision.HIGHEST
E, C, T, D, F = 16, 4, 128, 2048, 512
Q = 4
W = D // Q
MR = Q * C
RR = E * MR
R = E * C
K = 2 * R
CH = 64
NS = 2
SR = CH // NS
GAPS = ((2, 3, 3, 4, 4), (2, 3, 3, 4, 3))
STOPS = tuple(tuple(sum(g[i:]) for i in range(len(g) + 1)) for g in GAPS)
BETWEEN = tuple([(i, j) for i in range(1, len(g) + 1) for j in range(1, g[i - 1])] for g in GAPS)
REACH = max(max(g) for g in GAPS) - 1
OFFSETS = sorted(set(range(1, REACH + 1)) | set(GAPS[0]) | set(GAPS[1]))
SLICES = max(len(b) for b in BETWEEN)
STEPS = max(len(g) for g in GAPS)


def dot(a, b, dims=((1,), (0,)), precision=None):
    return lax.dot_general(a, b, (dims, ((), ())), preferred_element_type=F32, precision=precision)


def iota(shape, dim):
    return lax.broadcasted_iota(jnp.int32, shape, dim)


def kernel(nz, picked_h, gate_h, tok_h, og_h, win_h, wout_h,
           lo_h, tg_h, gg_h, gpi_h,
           picked, gate, tok, og, win, wout, lo, tg, gg, gpi,
           rows_s, sc_s, rows_r, sc_r, eo_s, ir_s, eo_r, ir_r, g_v,
           x_v, xt, hid, bp, perm, perm_t, a_hi, a_lo, a_one, xs, bpn, ms, mr,
           ld_sem, st_sem, in_ss, in_rs, out_ss, out_rs, sib_ss, sib_rs, m_ss, m_rs, x_ss, x_rs, b_ss, b_rs):
    me = lax.axis_index("expert")
    dp = lax.axis_index("dp")
    z, h = dp // 2, dp % 2
    even, odd = z * 2, z * 2 + 1

    def zdev(offset):
        return (me, lax.rem(z + offset + nz, nz) * 2 + h)

    barrier = pltpu.get_barrier_semaphore()

    def signal(dev):
        pl.semaphore_signal(barrier, inc=1, device_id=dev, device_id_type=MESH)

    def greet(k, _):
        e = lax.rem(me + k, E)
        signal((e, odd))
        signal((e, even))
        return 0

    lax.fori_loop(1, E, greet, 0)
    signal((me, z * 2 + (1 - h)))

    @pl.when(h == 1)
    def _():
        for off in OFFSETS:
            signal(zdev(off))
            signal(zdev(-off))

    pairs = [(picked_h, picked), (gate_h, gate), (tok_h, tok), (og_h, og), (win_h, win), (wout_h, wout)]
    loads = [pltpu.make_async_copy(s, d, ld_sem.at[i]) for i, (s, d) in enumerate(pairs)]
    for c in loads:
        c.start()

    sel_e = ((iota((RR, E), 0) >> 4) == iota((RR, E), 1)).astype(F32)
    is_c = (iota((RR, C), 0) & 3) == iota((RR, C), 1)
    diag = iota((RR, RR), 0) == iota((RR, RR), 1)
    loads[0].wait()
    loads[1].wait()
    pk4 = dot(sel_e, picked[...].astype(F32), NT, HIGH)
    w4 = dot(sel_e, gate[...], NT, HIGH)
    pk = jnp.sum(jnp.where(is_c, pk4, 0.0), axis=1, keepdims=True)
    w = jnp.sum(jnp.where(is_c, w4, 0.0), axis=1, keepdims=True)
    tgt = pk.astype(jnp.int32) + ((iota((RR, 1), 0) >> 2) & 3) * T
    gather = (iota((RR, Q * T), 1) == tgt).astype(F32).astype(BF)

    def quarters(ref):
        return jnp.concatenate([ref[:, q * W:(q + 1) * W] for q in range(Q)], axis=0)

    def block(i, base=0):
        return pl.ds(pl.multiple_of(base + i * MR, MR), MR)

    def send_in(k, src, dst):
        def copy(e):
            return pltpu.make_async_remote_copy(
                src_ref=src.at[block(e)], dst_ref=dst.at[block(me, h * RR)],
                send_sem=in_ss.at[k], recv_sem=in_rs.at[k, h],
                device_id=(e, odd), device_id_type=MESH)

        def send(i, _):
            copy(lax.rem(me + i, E)).start()
            return 0

        lax.fori_loop(1, E, send, 0)

        @pl.when(h == 0)
        def _():
            copy(me).start()

        @pl.when(h == 1)
        def _():
            dst[block(me, RR), :] = src[block(me), :]

    def wait_rows(ref, start, count, sem):
        part = ref.at[pl.ds(start, count)]
        pltpu.make_async_copy(part, part, sem).wait()

    loads[2].wait()
    rows_s[...] = dot(gather, quarters(tok)).astype(BF)
    loads[3].wait()
    grad_rows = dot(gather, quarters(og))
    sc_s[...] = (w * grad_rows).astype(BF)
    g_v[...] = grad_rows.astype(BF)

    @pl.when(h == 0)
    def _():
        pl.semaphore_wait(barrier, 2 * E - 1)

    @pl.when(h == 1)
    def _():
        pl.semaphore_wait(barrier, 2 * E - 1 + 2 * len(OFFSETS))

    send_in(0, rows_s, rows_r)
    send_in(1, sc_s, sc_r)

    i0, i1 = iota((RR, RR), 0), iota((RR, RR), 1)
    to_q = ((i0 >> 2) & 15) * MR + (i0 >> 6) * C + (i0 & 3)
    perm[...] = (i1 == to_q).astype(F32).astype(BF)
    to_q_t = ((i1 >> 2) & 15) * MR + (i1 >> 6) * C + (i1 & 3)
    perm_t[...] = (i0 == to_q_t).astype(F32).astype(BF)
    tgt_row = jnp.sum(jnp.where(diag, tgt.astype(F32), 0.0), axis=0, keepdims=True).astype(jnp.int32)
    w_row = jnp.sum(jnp.where(diag, w, 0.0), axis=0, keepdims=True)
    hit = iota((Q * T, RR), 0) == tgt_row
    a_one[...] = hit.astype(F32).astype(BF)
    w_hi = w_row.astype(BF).astype(F32)
    a_hi[...] = jnp.where(hit, w_hi, 0.0).astype(BF)
    a_lo[...] = jnp.where(hit, w_row - w_hi, 0.0).astype(BF)

    def combine_out():
        for q in range(Q):
            a = slice(q * T, (q + 1) * T)
            lo[:, q * W:(q + 1) * W] = (dot(a_hi[a, :], eo_r[...]) + dot(a_lo[a, :], eo_r[...])).astype(BF)
        stores[0].start()
        prod = jnp.sum(g_v[...].astype(F32) * eo_r[...].astype(F32), axis=1, keepdims=True)
        sel_t = ((iota((E, RR), 1) >> 4) == iota((E, RR), 0)).astype(F32)
        prod_row = jnp.sum(jnp.where(diag, prod, 0.0), axis=0, keepdims=True)
        by_c = jnp.where((iota((C, RR), 1) & 3) == iota((C, RR), 0), prod_row, 0.0)
        gg[...] = dot(by_c, sel_t, NT, HIGH)
        stores[2].start()

    def combine_grad():
        for q in range(Q):
            tg[:, q * W:(q + 1) * W] = dot(a_one[q * T:(q + 1) * T, :], ir_r[...]).astype(BF)
        stores[1].start()

    stores = [pltpu.make_async_copy(s, d, st_sem.at[i])
              for i, (s, d) in enumerate([(lo, lo_h), (tg, tg_h), (gg, gg_h)])]

    def to_sib(i, src, dst):
        return pltpu.make_async_remote_copy(
            src_ref=src, dst_ref=dst, send_sem=sib_ss.at[i], recv_sem=sib_rs.at[i],
            device_id=(me, z * 2 + (1 - h)), device_id_type=MESH)

    hid_copy = to_sib(0, hid, hid)
    bp_copy = to_sib(1, bp, bp)
    gpi_copy = to_sib(2, gpi.at[pl.ds(0, CH // 2)], gpi_h)
    gpi_own = pltpu.make_async_copy(gpi.at[pl.ds(CH // 2, CH // 2)], gpi_h, st_sem.at[3])

    def by_quarter(src, dst):
        for cs in range(2):
            xs = dot(perm[...], src[cs * RR:(cs + 1) * RR, :]).astype(BF)
            for q in range(Q):
                dst[q, cs * R:(cs + 1) * R, :] = xs[q * R:(q + 1) * R, :]

    def along(s, hops):
        return zdev(hops if s == 0 else -hops)

    def columns(s, d):
        t = lax.rem(z + (d if s == 0 else -d) + nz, nz)
        return pl.ds(pl.multiple_of(t * CH, CH), CH)

    @pl.when(h == 1)
    def _():
        wait_rows(rows_r, 0, RR, in_rs.at[0, 0])
        wait_rows(rows_r, RR, RR - MR, in_rs.at[0, 1])
        by_quarter(rows_r, x_v)
        loads[4].wait()
        pre = dot(x_v[0], win[0:W, :])
        for q in range(1, Q):
            pre += dot(x_v[q], win[q * W:(q + 1) * W, :])
        cdf = 0.5 * (1.0 + lax.erf(pre * (1.0 / math.sqrt(2.0))))
        hid[...] = (pre * cdf).astype(BF)
        hid_copy.start()
        slope = cdf + pre * (jnp.exp(-0.5 * pre * pre) * (1.0 / math.sqrt(2.0 * math.pi)))
        for q in range(Q):
            xt[q * W:(q + 1) * W, :] = x_v[q].T
        for s in range(2):
            for n, (i, j) in enumerate(BETWEEN[s]):
                pltpu.make_async_remote_copy(
                    src_ref=xt.at[columns(s, STOPS[s][i] + j)], dst_ref=xs.at[s, pl.ds(n * CH, CH)],
                    send_sem=x_ss.at[s], recv_sem=x_rs.at[s], device_id=along(s, j), device_id_type=MESH).start()
        loads[5].wait()
        wait_rows(sc_r, 0, RR, in_rs.at[1, 0])
        wait_rows(sc_r, RR, RR - MR, in_rs.at[1, 1])
        by_quarter(sc_r, x_v)
        back = dot(x_v[0], wout[:, 0:W], NT)
        for q in range(1, Q):
            back += dot(x_v[q], wout[:, q * W:(q + 1) * W], NT)
        bp[...] = (back * slope).astype(BF)
        bp_copy.start()

        def pass_on(s, j):
            return pltpu.make_async_remote_copy(
                src_ref=bpn.at[s, j - 1] if j else bp, dst_ref=bpn.at[s, j],
                send_sem=b_ss.at[s, j], recv_sem=b_rs.at[s, j], device_id=along(s, 1), device_id_type=MESH)

        def message(s, i, u):
            part = pl.ds(u * SR, SR)
            return pltpu.make_async_remote_copy(
                src_ref=ms.at[s, i, part], dst_ref=mr.at[s, i, part],
                send_sem=m_ss.at[s, i, u], recv_sem=m_rs.at[s, i, u],
                device_id=along(s, GAPS[s][i]), device_id_type=MESH)

        arrived = [0]

        def need(j):
            while arrived[0] < j:
                k = arrived[0]
                for s in range(2):
                    pass_on(s, k).wait_recv()
                    if k + 1 < REACH:
                        pass_on(s, k + 1).start()
                arrived[0] += 1

        def others(s, i):
            total = None
            for n, (k, j) in enumerate(BETWEEN[s]):
                if k == i:
                    need(j)
                    term = dot(xs[s, n * CH:(n + 1) * CH, :], bpn[s, j - 1])
                    total = term if total is None else total + term
            return total

        def add(total, s, i, u):
            message(s, i - 1, u).wait_recv()
            return total + mr[s, i - 1, u * SR:(u + 1) * SR, :].astype(F32)

        def stop(s, i):
            mine = dot(xt[columns(s, STOPS[s][i]), :], bp[...])
            if i:
                mine = mine + others(s, i)
            for u in range(NS):
                total = mine[u * SR:(u + 1) * SR]
                if i:
                    total = add(total, s, i, u)
                ms[s, i, u * SR:(u + 1) * SR, :] = total.astype(BF)
                message(s, i, u).start()

        for s in range(2):
            pass_on(s, 0).start()
        for s in range(2):
            stop(s, 0)
        for s in range(2):
            wait_rows(xs.at[s], 0, len(BETWEEN[s]) * CH, x_rs.at[s])
        for i in range(1, STEPS):
            for s in range(2):
                stop(s, i)
            if i == STEPS - 2:
                wait_rows(eo_r, 0, RR, out_rs.at[0])
                combine_out()
        wait_rows(ir_r, 0, RR, out_rs.at[1])
        combine_grad()

        mine = dot(xt[columns(0, 0), :], bp[...]) + others(0, STEPS) + others(1, STEPS)
        need(REACH)
        for u in range(NS):
            total = mine[u * SR:(u + 1) * SR]
            for s in range(2):
                total = add(total, s, STEPS, u)
            gpi[u * SR:(u + 1) * SR, :] = total
            if u == max(NS // 2 - 1, 0):
                gpi_copy.start()
        gpi_own.start()
        wait_rows(rows_s, 0, RR - MR, in_ss.at[0])
        wait_rows(sc_s, 0, RR - MR, in_ss.at[1])
        hid_copy.wait_send()
        bp_copy.wait_send()
        for s in range(2):
            wait_rows(xs.at[s], 0, len(BETWEEN[s]) * CH, x_ss.at[s])
            for j in range(REACH):
                pass_on(s, j).wait_send()
            for i in range(STEPS):
                for u in range(NS):
                    message(s, i, u).wait_send()
        gpi_copy.wait_send()
        gpi_own.wait()

    @pl.when(h == 0)
    def _():
        def send_out(k, src, dst):
            def copy(cs, e):
                return pltpu.make_async_remote_copy(
                    src_ref=src.at[block(e, cs * RR)], dst_ref=dst.at[block(me)],
                    send_sem=out_ss.at[k, cs], recv_sem=out_rs.at[k],
                    device_id=(e, z * 2 + cs), device_id_type=MESH)

            def send(i, _):
                e = lax.rem(me + i, E)
                copy(1, e).start()
                copy(0, e).start()
                return 0

            lax.fori_loop(1, E, send, 0)
            copy(1, me).start()
            dst[block(me), :] = src[block(me), :]

        def by_source(parts, dst):
            for cs in range(2):
                rows = jnp.concatenate([p[cs * R:(cs + 1) * R] for p in parts], axis=0)
                dst[cs * RR:(cs + 1) * RR, :] = dot(perm_t[...], rows).astype(BF)

        loads[4].wait()
        loads[5].wait()
        hid_copy.wait_recv()
        by_source([dot(hid[...], wout[:, q * W:(q + 1) * W]).astype(BF) for q in range(Q)], eo_s)
        send_out(0, eo_s, eo_r)
        bp_copy.wait_recv()
        by_source([dot(bp[...], win[q * W:(q + 1) * W, :], NT).astype(BF) for q in range(Q)], ir_s)
        send_out(1, ir_s, ir_r)
        wait_rows(eo_r, 0, RR - MR, out_rs.at[0])
        combine_out()
        wait_rows(ir_r, 0, RR - MR, out_rs.at[1])
        combine_grad()
        wait_rows(rows_s, 0, RR, in_ss.at[0])
        wait_rows(sc_s, 0, RR, in_ss.at[1])
        for k, src in enumerate((eo_s, ir_s)):
            wait_rows(src, 0, RR - MR, out_ss.at[k, 0])
            wait_rows(src, 0, RR, out_ss.at[k, 1])
        gpi_copy.wait_recv()

    for c in stores:
        c.wait()


def copy_out(a, b, c, d, oa, ob, oc, od, sem):
    copies = [pltpu.make_async_copy(s, t, sem.at[i]) for i, (s, t) in enumerate(((a, oa), (b, ob), (c, oc), (d, od)))]
    for x in copies:
        x.start()
    for x in copies:
        x.wait()


def body(nz, tokens, out_grad, proj_in, proj_out, picked, gate_values):
    hbm = pl.BlockSpec(memory_space=pltpu.HBM)
    vmem = pl.BlockSpec(memory_space=pltpu.VMEM)
    dma = pltpu.SemaphoreType.DMA

    def buf(*shape, dtype=BF):
        return pltpu.VMEM(shape, dtype)

    shapes = (
        jax.ShapeDtypeStruct((T, D), BF),
        jax.ShapeDtypeStruct((T, D), BF),
        jax.ShapeDtypeStruct((C, E), F32),
        jax.ShapeDtypeStruct((CH // 2, F), F32),
    )
    outs = pl.pallas_call(
        functools.partial(kernel, nz),
        out_shape=shapes,
        in_specs=[hbm] * 6,
        out_specs=(hbm,) * 4,
        scratch_shapes=[
            buf(C, E, dtype=jnp.int32), buf(C, E, dtype=F32), buf(T, D), buf(T, D), buf(D, F), buf(F, D),
            buf(T, D), buf(T, D), buf(C, E, dtype=F32), buf(CH, F, dtype=F32),
            buf(RR, W), buf(RR, W), buf(2 * RR, W), buf(2 * RR, W), buf(2 * RR, W), buf(2 * RR, W),
            buf(RR, W), buf(RR, W), buf(RR, W),
            buf(Q, K, W), buf(D, K), buf(K, F), buf(K, F), buf(RR, RR), buf(RR, RR),
            buf(Q * T, RR), buf(Q * T, RR), buf(Q * T, RR),
            buf(2, SLICES * CH, K), buf(2, REACH, K, F), buf(2, STEPS, CH, F), buf(2, STEPS, CH, F),
            dma((6,)), dma((4,)), dma((2,)), dma((2, 2)), dma((2, 2)), dma((2,)), dma((3,)), dma((3,)),
            dma((2, STEPS, NS)), dma((2, STEPS, NS)), dma((2,)), dma((2,)), dma((2, REACH)), dma((2, REACH)),
        ],
        compiler_params=pltpu.CompilerParams(
            collective_id=0, has_side_effects=True, vmem_limit_bytes=60 * 1024 * 1024),
        name="moe_layer",
    )(picked[0].T, gate_values[0].T, tokens, out_grad, proj_in[0], proj_out[0])
    lo, tg, gg, gpi = pl.pallas_call(
        copy_out, out_shape=shapes, in_specs=[vmem] * 4, out_specs=(hbm,) * 4,
        scratch_shapes=[dma((4,))], name="copy_out",
    )(*outs)
    return lo, tg, gg.T[None], gpi[None]


def solution(mesh):
    return jax.shard_map(
        functools.partial(body, mesh.shape["dp"] // 2),
        mesh=mesh,
        in_specs=(
            P(("expert", "dp"), None),
            P(("expert", "dp"), None),
            P("expert", None, None),
            P("expert", None, None),
            P(("expert", "dp"), None, None),
            P(("expert", "dp"), None, None),
        ),
        out_specs=(
            P(("expert", "dp"), None),
            P(("expert", "dp"), None),
            P(("expert", "dp"), None, None),
            P("expert", "dp", None),
        ),
        check_vma=False,
    )
```

```python
import functools
import math

import jax
import jax.numpy as jnp
from jax import lax
from jax.experimental import pallas as pl
from jax.experimental.pallas import tpu as pltpu
from jax.sharding import PartitionSpec as P

MESH = pl.DeviceIdType.MESH
BF = jnp.bfloat16
NT = ((1,), (1,))
F32 = jnp.float32
HIGH = lax.Precision.HIGHEST
E, C, T, D, F = 16, 4, 128, 2048, 512
Q = 4
W = D // Q
MR = Q * C
RR = E * MR
R = E * C
K = 2 * R
CH = 64
NS = 2
SR = CH // NS
GAPS = ((2, 3, 3, 4, 4), (2, 3, 3, 4, 3))
STOPS = tuple(tuple(sum(g[i:]) for i in range(len(g) + 1)) for g in GAPS)
BETWEEN = tuple([(i, j) for i in range(1, len(g) + 1) for j in range(1, g[i - 1])] for g in GAPS)
REACH = max(max(g) for g in GAPS) - 1
OFFSETS = sorted(set(range(1, REACH + 1)) | set(GAPS[0]) | set(GAPS[1]))
SLICES = max(len(b) for b in BETWEEN)
STEPS = max(len(g) for g in GAPS)


def dot(a, b, dims=((1,), (0,)), precision=None):
    return lax.dot_general(a, b, (dims, ((), ())), preferred_element_type=F32, precision=precision)


def iota(shape, dim):
    return lax.broadcasted_iota(jnp.int32, shape, dim)


def kernel(nz, picked_h, gate_h, tok_h, og_h, win_h, wout_h,
           lo_h, tg_h, gg_h, gpi_h,
           picked, gate, tok, og, win, wout, lo, tg, gg, gpi,
           rows_s, sc_s, rows_r, sc_r, eo_s, ir_s, eo_r, ir_r, g_v,
           x_v, xt, hid, bp, perm, perm_t, a_hi, a_lo, a_one, xs, bpn, ms, mr,
           ld_sem, st_sem, in_ss, in_rs, out_ss, out_rs, sib_ss, sib_rs, m_ss, m_rs, x_ss, x_rs, b_ss, b_rs):
    me = lax.axis_index("expert")
    dp = lax.axis_index("dp")
    z, h = dp // 2, dp % 2
    even, odd = z * 2, z * 2 + 1

    def zdev(offset):
        return (me, lax.rem(z + offset + nz, nz) * 2 + h)

    barrier = pltpu.get_barrier_semaphore()

    def signal(dev):
        pl.semaphore_signal(barrier, inc=1, device_id=dev, device_id_type=MESH)

    def greet(k, _):
        e = lax.rem(me + k, E)
        signal((e, odd))
        signal((e, even))
        return 0

    lax.fori_loop(1, E, greet, 0)
    signal((me, z * 2 + (1 - h)))

    @pl.when(h == 1)
    def _():
        for off in OFFSETS:
            signal(zdev(off))
            signal(zdev(-off))

    pairs = [(picked_h, picked), (gate_h, gate), (tok_h, tok), (og_h, og), (win_h, win), (wout_h, wout)]
    loads = [pltpu.make_async_copy(s, d, ld_sem.at[i]) for i, (s, d) in enumerate(pairs)]
    for c in loads:
        c.start()

    sel_e = ((iota((RR, E), 0) >> 4) == iota((RR, E), 1)).astype(F32)
    is_c = (iota((RR, C), 0) & 3) == iota((RR, C), 1)
    diag = iota((RR, RR), 0) == iota((RR, RR), 1)
    loads[0].wait()
    loads[1].wait()
    pk4 = dot(sel_e, picked[...].astype(F32), NT, HIGH)
    w4 = dot(sel_e, gate[...], NT, HIGH)
    pk = jnp.sum(jnp.where(is_c, pk4, 0.0), axis=1, keepdims=True)
    w = jnp.sum(jnp.where(is_c, w4, 0.0), axis=1, keepdims=True)
    tgt = pk.astype(jnp.int32) + ((iota((RR, 1), 0) >> 2) & 3) * T
    gather = (iota((RR, Q * T), 1) == tgt).astype(F32).astype(BF)

    def quarters(ref):
        return jnp.concatenate([ref[:, q * W:(q + 1) * W] for q in range(Q)], axis=0)

    def block(i, base=0):
        return pl.ds(pl.multiple_of(base + i * MR, MR), MR)

    def send_in(k, src, dst):
        def copy(e):
            return pltpu.make_async_remote_copy(
                src_ref=src.at[block(e)], dst_ref=dst.at[block(me, h * RR)],
                send_sem=in_ss.at[k], recv_sem=in_rs.at[k, h],
                device_id=(e, odd), device_id_type=MESH)

        def send(i, _):
            copy(lax.rem(me + i, E)).start()
            return 0

        lax.fori_loop(1, E, send, 0)

        @pl.when(h == 0)
        def _():
            copy(me).start()

        @pl.when(h == 1)
        def _():
            dst[block(me, RR), :] = src[block(me), :]

    def wait_rows(ref, start, count, sem):
        part = ref.at[pl.ds(start, count)]
        pltpu.make_async_copy(part, part, sem).wait()

    loads[2].wait()
    rows_s[...] = dot(gather, quarters(tok)).astype(BF)
    loads[3].wait()
    grad_rows = dot(gather, quarters(og))
    sc_s[...] = (w * grad_rows).astype(BF)
    g_v[...] = grad_rows.astype(BF)

    @pl.when(h == 0)
    def _():
        pl.semaphore_wait(barrier, 2 * E - 1)

    @pl.when(h == 1)
    def _():
        pl.semaphore_wait(barrier, 2 * E - 1 + 2 * len(OFFSETS))

    send_in(0, rows_s, rows_r)
    send_in(1, sc_s, sc_r)

    i0, i1 = iota((RR, RR), 0), iota((RR, RR), 1)
    to_q = ((i0 >> 2) & 15) * MR + (i0 >> 6) * C + (i0 & 3)
    perm[...] = (i1 == to_q).astype(F32).astype(BF)
    to_q_t = ((i1 >> 2) & 15) * MR + (i1 >> 6) * C + (i1 & 3)
    perm_t[...] = (i0 == to_q_t).astype(F32).astype(BF)
    tgt_row = jnp.sum(jnp.where(diag, tgt.astype(F32), 0.0), axis=0, keepdims=True).astype(jnp.int32)
    w_row = jnp.sum(jnp.where(diag, w, 0.0), axis=0, keepdims=True)
    hit = iota((Q * T, RR), 0) == tgt_row
    a_one[...] = hit.astype(F32).astype(BF)
    w_hi = w_row.astype(BF).astype(F32)
    a_hi[...] = jnp.where(hit, w_hi, 0.0).astype(BF)
    a_lo[...] = jnp.where(hit, w_row - w_hi, 0.0).astype(BF)

    def combine_out():
        for q in range(Q):
            a = slice(q * T, (q + 1) * T)
            lo[:, q * W:(q + 1) * W] = (dot(a_hi[a, :], eo_r[...]) + dot(a_lo[a, :], eo_r[...])).astype(BF)
        stores[0].start()
        prod = jnp.sum(g_v[...].astype(F32) * eo_r[...].astype(F32), axis=1, keepdims=True)
        sel_t = ((iota((E, RR), 1) >> 4) == iota((E, RR), 0)).astype(F32)
        prod_row = jnp.sum(jnp.where(diag, prod, 0.0), axis=0, keepdims=True)
        by_c = jnp.where((iota((C, RR), 1) & 3) == iota((C, RR), 0), prod_row, 0.0)
        gg[...] = dot(by_c, sel_t, NT, HIGH)
        stores[2].start()

    def combine_grad():
        for q in range(Q):
            tg[:, q * W:(q + 1) * W] = dot(a_one[q * T:(q + 1) * T, :], ir_r[...]).astype(BF)
        stores[1].start()

    stores = [pltpu.make_async_copy(s, d, st_sem.at[i])
              for i, (s, d) in enumerate([(lo, lo_h), (tg, tg_h), (gg, gg_h)])]

    def to_sib(i, src, dst):
        return pltpu.make_async_remote_copy(
            src_ref=src, dst_ref=dst, send_sem=sib_ss.at[i], recv_sem=sib_rs.at[i],
            device_id=(me, z * 2 + (1 - h)), device_id_type=MESH)

    hid_copy = to_sib(0, hid, hid)
    bp_copy = to_sib(1, bp, bp)
    gpi_copy = to_sib(2, gpi.at[pl.ds(0, CH // 2)], gpi_h)
    gpi_own = pltpu.make_async_copy(gpi.at[pl.ds(CH // 2, CH // 2)], gpi_h, st_sem.at[3])

    def by_quarter(src, dst):
        for cs in range(2):
            xs = dot(perm[...], src[cs * RR:(cs + 1) * RR, :]).astype(BF)
            for q in range(Q):
                dst[q, cs * R:(cs + 1) * R, :] = xs[q * R:(q + 1) * R, :]

    def along(s, hops):
        return zdev(hops if s == 0 else -hops)

    def columns(s, d):
        t = lax.rem(z + (d if s == 0 else -d) + nz, nz)
        return pl.ds(pl.multiple_of(t * CH, CH), CH)

    @pl.when(h == 1)
    def _():
        wait_rows(rows_r, 0, RR, in_rs.at[0, 0])
        wait_rows(rows_r, RR, RR - MR, in_rs.at[0, 1])
        by_quarter(rows_r, x_v)
        loads[4].wait()
        pre = dot(x_v[0], win[0:W, :])
        for q in range(1, Q):
            pre += dot(x_v[q], win[q * W:(q + 1) * W, :])
        cdf = 0.5 * (1.0 + lax.erf(pre * (1.0 / math.sqrt(2.0))))
        hid[...] = (pre * cdf).astype(BF)
        hid_copy.start()
        slope = cdf + pre * (jnp.exp(-0.5 * pre * pre) * (1.0 / math.sqrt(2.0 * math.pi)))
        for q in range(Q):
            xt[q * W:(q + 1) * W, :] = x_v[q].T
        for s in range(2):
            for n, (i, j) in enumerate(BETWEEN[s]):
                pltpu.make_async_remote_copy(
                    src_ref=xt.at[columns(s, STOPS[s][i] + j)], dst_ref=xs.at[s, pl.ds(n * CH, CH)],
                    send_sem=x_ss.at[s], recv_sem=x_rs.at[s], device_id=along(s, j), device_id_type=MESH).start()
        loads[5].wait()
        wait_rows(sc_r, 0, RR, in_rs.at[1, 0])
        wait_rows(sc_r, RR, RR - MR, in_rs.at[1, 1])
        by_quarter(sc_r, x_v)
        back = dot(x_v[0], wout[:, 0:W], NT)
        for q in range(1, Q):
            back += dot(x_v[q], wout[:, q * W:(q + 1) * W], NT)
        bp[...] = (back * slope).astype(BF)
        bp_copy.start()

        def pass_on(s, j):
            return pltpu.make_async_remote_copy(
                src_ref=bpn.at[s, j - 1] if j else bp, dst_ref=bpn.at[s, j],
                send_sem=b_ss.at[s, j], recv_sem=b_rs.at[s, j], device_id=along(s, 1), device_id_type=MESH)

        def message(s, i, u):
            part = pl.ds(u * SR, SR)
            return pltpu.make_async_remote_copy(
                src_ref=ms.at[s, i, part], dst_ref=mr.at[s, i, part],
                send_sem=m_ss.at[s, i, u], recv_sem=m_rs.at[s, i, u],
                device_id=along(s, GAPS[s][i]), device_id_type=MESH)

        arrived = [0]

        def need(j):
            while arrived[0] < j:
                k = arrived[0]
                for s in range(2):
                    pass_on(s, k).wait_recv()
                    if k + 1 < REACH:
                        pass_on(s, k + 1).start()
                arrived[0] += 1

        def others(s, i):
            total = None
            for n, (k, j) in enumerate(BETWEEN[s]):
                if k == i:
                    need(j)
                    term = dot(xs[s, n * CH:(n + 1) * CH, :], bpn[s, j - 1])
                    total = term if total is None else total + term
            return total

        def add(total, s, i, u):
            message(s, i - 1, u).wait_recv()
            return total + mr[s, i - 1, u * SR:(u + 1) * SR, :].astype(F32)

        def stop(s, i):
            mine = dot(xt[columns(s, STOPS[s][i]), :], bp[...])
            if i:
                mine = mine + others(s, i)
            for u in range(NS):
                total = mine[u * SR:(u + 1) * SR]
                if i:
                    total = add(total, s, i, u)
                ms[s, i, u * SR:(u + 1) * SR, :] = total.astype(BF)
                message(s, i, u).start()

        for s in range(2):
            stop(s, 0)
        for s in range(2):
            pass_on(s, 0).start()
        for s in range(2):
            wait_rows(xs.at[s], 0, len(BETWEEN[s]) * CH, x_rs.at[s])
        for i in range(1, STEPS):
            for s in range(2):
                stop(s, i)
            if i == STEPS - 2:
                wait_rows(eo_r, 0, RR, out_rs.at[0])
                combine_out()
        wait_rows(ir_r, 0, RR, out_rs.at[1])
        combine_grad()

        mine = dot(xt[columns(0, 0), :], bp[...]) + others(0, STEPS) + others(1, STEPS)
        need(REACH)
        for u in range(NS):
            total = mine[u * SR:(u + 1) * SR]
            for s in range(2):
                total = add(total, s, STEPS, u)
            gpi[u * SR:(u + 1) * SR, :] = total
            if u == max(NS // 2 - 1, 0):
                gpi_copy.start()
        gpi_own.start()
        wait_rows(rows_s, 0, RR - MR, in_ss.at[0])
        wait_rows(sc_s, 0, RR - MR, in_ss.at[1])
        hid_copy.wait_send()
        bp_copy.wait_send()
        for s in range(2):
            wait_rows(xs.at[s], 0, len(BETWEEN[s]) * CH, x_ss.at[s])
            for j in range(REACH):
                pass_on(s, j).wait_send()
            for i in range(STEPS):
                for u in range(NS):
                    message(s, i, u).wait_send()
        gpi_copy.wait_send()
        gpi_own.wait()

    @pl.when(h == 0)
    def _():
        def send_out(k, src, dst):
            def copy(cs, e):
                return pltpu.make_async_remote_copy(
                    src_ref=src.at[block(e, cs * RR)], dst_ref=dst.at[block(me)],
                    send_sem=out_ss.at[k, cs], recv_sem=out_rs.at[k],
                    device_id=(e, z * 2 + cs), device_id_type=MESH)

            def send(i, _):
                e = lax.rem(me + i, E)
                copy(1, e).start()
                copy(0, e).start()
                return 0

            lax.fori_loop(1, E, send, 0)
            copy(1, me).start()
            dst[block(me), :] = src[block(me), :]

        def by_source(parts, dst):
            for cs in range(2):
                rows = jnp.concatenate([p[cs * R:(cs + 1) * R] for p in parts], axis=0)
                dst[cs * RR:(cs + 1) * RR, :] = dot(perm_t[...], rows).astype(BF)

        loads[4].wait()
        loads[5].wait()
        hid_copy.wait_recv()
        by_source([dot(hid[...], wout[:, q * W:(q + 1) * W]).astype(BF) for q in range(Q)], eo_s)
        send_out(0, eo_s, eo_r)
        bp_copy.wait_recv()
        by_source([dot(bp[...], win[q * W:(q + 1) * W, :], NT).astype(BF) for q in range(Q)], ir_s)
        send_out(1, ir_s, ir_r)
        wait_rows(eo_r, 0, RR - MR, out_rs.at[0])
        combine_out()
        wait_rows(ir_r, 0, RR - MR, out_rs.at[1])
        combine_grad()
        wait_rows(rows_s, 0, RR, in_ss.at[0])
        wait_rows(sc_s, 0, RR, in_ss.at[1])
        for k, src in enumerate((eo_s, ir_s)):
            wait_rows(src, 0, RR - MR, out_ss.at[k, 0])
            wait_rows(src, 0, RR, out_ss.at[k, 1])
        gpi_copy.wait_recv()

    for c in stores:
        c.wait()


def copy_out(a, b, c, d, oa, ob, oc, od, sem):
    copies = [pltpu.make_async_copy(s, t, sem.at[i]) for i, (s, t) in enumerate(((a, oa), (b, ob), (c, oc), (d, od)))]
    for x in copies:
        x.start()
    for x in copies:
        x.wait()


def body(nz, tokens, out_grad, proj_in, proj_out, picked, gate_values):
    hbm = pl.BlockSpec(memory_space=pltpu.HBM)
    vmem = pl.BlockSpec(memory_space=pltpu.VMEM)
    dma = pltpu.SemaphoreType.DMA

    def buf(*shape, dtype=BF):
        return pltpu.VMEM(shape, dtype)

    shapes = (
        jax.ShapeDtypeStruct((T, D), BF),
        jax.ShapeDtypeStruct((T, D), BF),
        jax.ShapeDtypeStruct((C, E), F32),
        jax.ShapeDtypeStruct((CH // 2, F), F32),
    )
    outs = pl.pallas_call(
        functools.partial(kernel, nz),
        out_shape=shapes,
        in_specs=[hbm] * 6,
        out_specs=(hbm,) * 4,
        scratch_shapes=[
            buf(C, E, dtype=jnp.int32), buf(C, E, dtype=F32), buf(T, D), buf(T, D), buf(D, F), buf(F, D),
            buf(T, D), buf(T, D), buf(C, E, dtype=F32), buf(CH, F, dtype=F32),
            buf(RR, W), buf(RR, W), buf(2 * RR, W), buf(2 * RR, W), buf(2 * RR, W), buf(2 * RR, W),
            buf(RR, W), buf(RR, W), buf(RR, W),
            buf(Q, K, W), buf(D, K), buf(K, F), buf(K, F), buf(RR, RR), buf(RR, RR),
            buf(Q * T, RR), buf(Q * T, RR), buf(Q * T, RR),
            buf(2, SLICES * CH, K), buf(2, REACH, K, F), buf(2, STEPS, CH, F), buf(2, STEPS, CH, F),
            dma((6,)), dma((4,)), dma((2,)), dma((2, 2)), dma((2, 2)), dma((2,)), dma((3,)), dma((3,)),
            dma((2, STEPS, NS)), dma((2, STEPS, NS)), dma((2,)), dma((2,)), dma((2, REACH)), dma((2, REACH)),
        ],
        compiler_params=pltpu.CompilerParams(
            collective_id=0, has_side_effects=True, vmem_limit_bytes=60 * 1024 * 1024),
        name="moe_layer",
    )(picked[0].T, gate_values[0].T, tokens, out_grad, proj_in[0], proj_out[0])
    lo, tg, gg, gpi = pl.pallas_call(
        copy_out, out_shape=shapes, in_specs=[vmem] * 4, out_specs=(hbm,) * 4,
        scratch_shapes=[dma((4,))], name="copy_out",
    )(*outs)
    return lo, tg, gg.T[None], gpi[None]


def solution(mesh):
    return jax.shard_map(
        functools.partial(body, mesh.shape["dp"] // 2),
        mesh=mesh,
        in_specs=(
            P(("expert", "dp"), None),
            P(("expert", "dp"), None),
            P("expert", None, None),
            P("expert", None, None),
            P(("expert", "dp"), None, None),
            P(("expert", "dp"), None, None),
        ),
        out_specs=(
            P(("expert", "dp"), None),
            P(("expert", "dp"), None),
            P(("expert", "dp"), None, None),
            P("expert", "dp", None),
        ),
        check_vma=False,
    )
```
